32 devices in a mesh: grp: 2 (over x), tp: 8 (over z, y), dp: 2 (over core).
Axes of the slice: x: 2, y: 2, z: 4, core: 2. Of those that a mesh axis runs over, the one named last changes fastest.
Arguments:
- tokens: bfloat16 [512, 4096], P(('grp', 'dp'), 'tp'), parts along dimension 0, may hold values from -6 to 6
- cotangent: bfloat16 [512, 4096], P(('grp', 'dp'), 'tp'), parts along dimension 0, may hold values from -6 to 6
- w_gate: bfloat16 [4096, 16384], P('dp', 'tp'), may hold values from -0.09375 to 0.09375
- w_up: bfloat16 [4096, 16384], P('dp', 'tp'), may hold values from -0.09375 to 0.09375
- w_down: bfloat16 [16384, 4096], P('tp', 'dp'), may hold values from -0.046875 to 0.046875
- gate_mask: int32 [32, 128], P(None, 'tp'), may hold values from 0 to 1, as said below
- up_mask: int32 [32, 128], P(None, 'tp'), may hold values from 0 to 1, as said below
- down_mask: int32 [128, 32], P('tp'), may hold values from 0 to 1, as said below
Outputs:
- layer_out: bfloat16 [512, 4096], P(('grp', 'dp'), 'tp'), parts along dimension 0
- input_grad: bfloat16 [512, 4096], P(('grp', 'dp'), 'tp'), parts along dimension 0
- gate_grad: bfloat16 [8192, 16384], P(('grp', 'dp'), 'tp'), parts along dimension 0
- up_grad: bfloat16 [8192, 16384], P(('grp', 'dp'), 'tp'), parts along dimension 0
- down_grad: bfloat16 [32768, 4096], P(('grp', 'tp'), 'dp'), parts along dimension 0
The draws below stay inside these ranges and needn't reach their ends.
There are 2 independent parts, one for each index of `grp`. The reference program is written for one: setup_inputs(seed, part) draws one part's arguments, and reference() takes and returns one part's arrays. A program takes and returns all parts, laid end to end along the dimension named above; an argument that names none is the same for every part. Nothing has to cross between parts.
Inputs may be any that keep to these rules, and one draw needn't show every extreme that they name: `gate_mask`: 1 keeps a 128 x 128 block of the weight, 0 sets it to zero. `up_mask`: 1 keeps a 128 x 128 block of the weight, 0 sets it to zero. `down_mask`: 1 keeps a 128 x 128 block of the weight, 0 sets it to zero.
All inputs are finite; a program needn't handle non-finite values.
Results may differ from the reference program's by a relative error of at most 0.0059.
Values may be sent and summed in bfloat16 or wider, within the bound.
No kernel may reach another device: no remote copies, remote signals or barrier semaphores. Data moves between devices by JAX's collectives and lax.ppermute only.
A program may use at most 320 MiB of HBM per device.

```python
import jax
import jax.numpy as jnp
from jax import lax

D = 4096
FF = 16384
BLK = 128
TOK_DEV = 128
TOKENS = 256
N_DP = 2


def mask_blocks(key, rows_count, cols_count, hidden_dim):
    hidden_blocks = FF // BLK
    shape = (rows_count, cols_count)
    place = jax.lax.broadcasted_iota(jnp.int32, shape, hidden_dim)
    limit = 250 + 500 * place // max(hidden_blocks - 1, 1)
    values = jax.random.randint(key, shape, 0, 1000)
    return (values < limit).astype(jnp.int32)


def draw_gate_mask(key, part):
    key = jax.random.fold_in(key, 11)
    return mask_blocks(key, D // BLK, FF // BLK, 1)


def draw_up_mask(key, part):
    key = jax.random.fold_in(key, 23)
    return mask_blocks(key, D // BLK, FF // BLK, 1)


def draw_down_mask(key, part):
    key = jax.random.fold_in(key, 37)
    return mask_blocks(key, FF // BLK, D // BLK, 0)


def block_levels(stream_key, dims, cuts, least, top_value):
    loudness = 1.0
    for axis_at, blocks in cuts:
        heights = jax.random.uniform(jax.random.fold_in(jax.random.fold_in(stream_key, 6), axis_at), (blocks,), jnp.float32, least / len(cuts), top_value / len(cuts))
        loudness = loudness * jnp.repeat(jnp.exp(heights), dims[axis_at] // blocks).reshape((-1,) + (1,) * (len(dims) - 1 - axis_at))
    return loudness


def noise(stream_key, shape, spread, reach, shards=(), kind=jnp.bfloat16):
    result = spread * jax.random.normal(stream_key, shape, jnp.float32)
    if shards:
        result = result * block_levels(stream_key, shape, shards, -0.22, 0.18)
    return jnp.clip(result, -reach, reach).astype(kind)


def setup_inputs(seed: int = 0, part: int = 0) -> dict:
    streams_of = jax.random.split(jax.random.key(seed), 9)
    part_splits = jax.random.split(jax.random.fold_in(streams_of[8], part), 9)
    return {
        "tokens": noise(part_splits[0], (TOKENS, D), 1.0, 6.0, ((0, 2), (1, 8))),
        "cotangent": noise(part_splits[1], (TOKENS, D), 1.0, 6.0, ((0, 2), (1, 8))),
        "w_gate": noise(streams_of[2], (D, FF), D ** -0.5, 0.09375, ((0, 2), (1, 8))),
        "w_up": noise(streams_of[3], (D, FF), D ** -0.5, 0.09375, ((0, 2), (1, 8))),
        "w_down": noise(streams_of[4], (FF, D), FF ** -0.5, 0.046875, ((0, 8), (1, 2))),
        "gate_mask": draw_gate_mask(jax.random.fold_in(streams_of[8], 71), part),
        "up_mask": draw_up_mask(jax.random.fold_in(streams_of[8], 71), part),
        "down_mask": draw_down_mask(jax.random.fold_in(streams_of[8], 71), part),
    }


def expand_blocks(block_mask, out_type):
    rows_blocks, cols_blocks = block_mask.shape
    grown = jnp.broadcast_to(block_mask[:, None, :, None].astype(out_type), (rows_blocks, BLK, cols_blocks, BLK))
    return grown.reshape(rows_blocks * BLK, cols_blocks * BLK)


def reference(tokens, cotangent, w_gate, w_up, w_down, gate_mask, up_mask, down_mask):
    gate_used = w_gate * expand_blocks(gate_mask, w_gate.dtype)
    up_used = w_up * expand_blocks(up_mask, w_up.dtype)
    down_used = w_down * expand_blocks(down_mask, w_down.dtype)
    gate = jnp.dot(tokens, gate_used, preferred_element_type=jnp.float32)
    up_value = jnp.dot(tokens, up_used, preferred_element_type=jnp.float32)
    gate_sigmoid = jax.nn.sigmoid(gate)
    hidden = (gate * gate_sigmoid * up_value).astype(jnp.bfloat16)
    layer_out = jnp.dot(hidden, down_used, preferred_element_type=jnp.float32).astype(jnp.bfloat16)
    hidden_grad = jnp.dot(cotangent, down_used.T, preferred_element_type=jnp.float32)
    gate_delta = (hidden_grad * up_value * gate_sigmoid * (1.0 + gate * (1.0 - gate_sigmoid))).astype(jnp.bfloat16)
    up_delta = (hidden_grad * gate * gate_sigmoid).astype(jnp.bfloat16)
    input_grad = (jnp.dot(gate_delta, gate_used.T, preferred_element_type=jnp.float32)
                  + jnp.dot(up_delta, up_used.T, preferred_element_type=jnp.float32)).astype(jnp.bfloat16)
    gate_keep = expand_blocks(gate_mask, jnp.float32)
    up_keep = expand_blocks(up_mask, jnp.float32)
    down_keep = expand_blocks(down_mask, jnp.float32)
    gate_total = jnp.zeros(w_gate.shape, jnp.float32)
    up_total = jnp.zeros(w_up.shape, jnp.float32)
    down_total = jnp.zeros(w_down.shape, jnp.float32)
    for shard in range(N_DP):
        first = shard * TOK_DEV
        rows_in = tokens[first:first + TOK_DEV]
        term_gate = jnp.dot(rows_in.T, gate_delta[first:first + TOK_DEV], preferred_element_type=jnp.float32) * gate_keep
        term_up = jnp.dot(rows_in.T, up_delta[first:first + TOK_DEV], preferred_element_type=jnp.float32) * up_keep
        term_down = jnp.dot(hidden[first:first + TOK_DEV].T, cotangent[first:first + TOK_DEV], preferred_element_type=jnp.float32) * down_keep
        term_gate = lax.optimization_barrier(term_gate.astype(jnp.bfloat16))
        term_up = lax.optimization_barrier(term_up.astype(jnp.bfloat16))
        term_down = lax.optimization_barrier(term_down.astype(jnp.bfloat16))
        gate_total = gate_total + term_gate.astype(jnp.float32)
        up_total = up_total + term_up.astype(jnp.float32)
        down_total = down_total + term_down.astype(jnp.float32)
    return (layer_out, input_grad, gate_total.astype(jnp.bfloat16),
            up_total.astype(jnp.bfloat16), down_total.astype(jnp.bfloat16))
```

```python
import functools

import jax
import jax.numpy as jnp
from jax import lax
from jax.experimental import pallas as pl
from jax.experimental.pallas import tpu as pltpu
from jax.sharding import PartitionSpec as P

BLK = 128
BF16 = jnp.bfloat16
F32 = jnp.float32
VMEM_LIMIT = 48 * 1024 * 1024
NN = (((1,), (0,)), ((), ()))
NT = (((1,), (1,)), ((), ()))


def dot(left, right, dims):
    return lax.dot_general(left, right, dims, preferred_element_type=F32)


def masked(weight, keep):
    rows, cols = weight.shape
    kept = weight.reshape(rows // BLK, BLK, cols) * keep.astype(weight.dtype)
    return kept.reshape(rows, cols)


def whole(shape):
    return pl.BlockSpec(shape, lambda *_: (0,) * len(shape))


def call(body, grid, in_specs, out_specs, out_shape, scratch, flops, name):
    return pl.pallas_call(
        body,
        grid_spec=pltpu.PrefetchScalarGridSpec(
            num_scalar_prefetch=1,
            grid=grid,
            in_specs=in_specs,
            out_specs=out_specs,
            scratch_shapes=scratch,
        ),
        out_shape=out_shape,
        compiler_params=pltpu.CompilerParams(vmem_limit_bytes=VMEM_LIMIT),
        cost_estimate=pl.CostEstimate(flops=flops, bytes_accessed=flops // 256, transcendentals=0),
        name=name,
    )


def collect(blocks, lhs, turn, half):
    rows, feats = blocks[0].shape
    for k, block in enumerate(blocks):
        place = pl.multiple_of(((k % half) ^ turn) * feats, feats)
        lhs[pl.ds((k // half) * rows, rows), pl.ds(place, feats)] = block[...]


def forward_body(half, turn_ref, *refs):
    blocks, (wg, wu, mg, mu) = refs[: 2 * half], refs[2 * half : 2 * half + 4]
    gate, gate_out, up, up_out, lhs = refs[2 * half + 4 :]

    @pl.when(pl.program_id(0) == 0)
    def _():
        collect(blocks, lhs, turn_ref[0], half)

    for weight, keep, own, out in ((wg, mg, gate, gate_out), (wu, mu, up, up_out)):
        part = dot(lhs[...], masked(weight[...], keep[...]), NN)
        own[...] = part
        out[...] = part.astype(BF16)


def forward(turn, blocks, w_gate, w_up, keep_gate, keep_up, half):
    rows, feats = blocks[0].shape
    depth, width = w_gate.shape
    tile = min(512, width)
    weight = pl.BlockSpec((depth, tile), lambda i, s: (0, i))
    keep = pl.BlockSpec((depth // BLK, 1, tile), lambda i, s: (0, 0, i))
    part = pl.BlockSpec((2 * rows, tile), lambda i, s: (0, i))
    return call(
        functools.partial(forward_body, half),
        (width // tile,),
        [whole((rows, feats))] * (2 * half) + [weight, weight, keep, keep],
        [part] * 4 + [whole((2 * rows, depth))],
        [jax.ShapeDtypeStruct((2 * rows, width), t) for t in (F32, BF16, F32, BF16)]
        + [jax.ShapeDtypeStruct((2 * rows, depth), BF16)],
        [],
        8 * rows * depth * width,
        "forward",
    )(turn, *blocks, w_gate, w_up, keep_gate, keep_up)


def hidden_grad_body(half, turn_ref, *refs):
    blocks, (wd, md) = refs[: 2 * half], refs[2 * half : 2 * half + 2]
    own, out, lhs = refs[2 * half + 2 :]

    @pl.when(pl.program_id(0) == 0)
    def _():
        collect(blocks, lhs, turn_ref[0], half)

    part = dot(lhs[...], masked(wd[...], md[...]), NT)
    own[...] = part
    out[...] = part.astype(BF16)


def hidden_grads(turn, blocks, w_down, keep_down, half):
    rows, feats = blocks[0].shape
    width, depth = w_down.shape
    tile = min(512, width)
    part = pl.BlockSpec((2 * rows, tile), lambda i, s: (0, i))
    return call(
        functools.partial(hidden_grad_body, half),
        (width // tile,),
        [whole((rows, feats))] * (2 * half)
        + [
            pl.BlockSpec((tile, depth), lambda i, s: (i, 0)),
            pl.BlockSpec((tile // BLK, 1, depth), lambda i, s: (i, 0, 0)),
        ],
        [part] * 2 + [whole((2 * rows, depth))],
        [jax.ShapeDtypeStruct((2 * rows, width), t) for t in (F32, BF16)]
        + [jax.ShapeDtypeStruct((2 * rows, depth), BF16)],
        [],
        4 * rows * depth * width,
        "hidden_grads",
    )(turn, *blocks, w_down, keep_down)


def put_blocks(part, blocks, half):
    rows = blocks[0].shape[0]
    step = pl.program_id(0)
    for j in range(half):

        @pl.when(step == j)
        def _(j=j):
            for group in range(2):
                blocks[group * half + j][...] = part[group * rows : (group + 1) * rows].astype(BF16)


def output_body(half, turn_ref, gate, gate_in, up, up_in, wd, md, *refs):
    blocks, hidden = refs[: 2 * half], refs[2 * half]

    @pl.when(pl.program_id(0) == 0)
    def _():
        gate_all = gate[...] + gate_in[...].astype(F32)
        up_all = up[...] + up_in[...].astype(F32)
        hidden[...] = (gate_all * jax.nn.sigmoid(gate_all) * up_all).astype(BF16)

    put_blocks(dot(hidden[...], masked(wd[...], md[...]), NN), blocks, half)


def outputs(turn, gate, gate_in, up, up_in, w_down, keep_down, half):
    rows, width = gate.shape
    rows = rows // 2
    depth = w_down.shape[1]
    feats = depth // half
    return call(
        functools.partial(output_body, half),
        (half,),
        [whole(gate.shape)] * 4
        + [
            pl.BlockSpec((width, feats), lambda i, s: (0, i ^ s[0])),
            pl.BlockSpec((width // BLK, 1, feats), lambda i, s: (0, 0, i ^ s[0])),
        ],
        [whole((rows, feats))] * (2 * half) + [whole(gate.shape)],
        [jax.ShapeDtypeStruct((rows, feats), BF16)] * (2 * half)
        + [jax.ShapeDtypeStruct(gate.shape, BF16)],
        [],
        4 * rows * depth * width,
        "outputs",
    )(turn, gate, gate_in, up, up_in, w_down, keep_down)


def input_grad_body(half, turn_ref, gate, gate_in, up, up_in, grad, grad_in, wg, wu, mg, mu, *refs):
    blocks, (gate_delta, up_delta) = refs[: 2 * half], refs[2 * half :]

    @pl.when(pl.program_id(0) == 0)
    def _():
        gate_all = gate[...] + gate_in[...].astype(F32)
        up_all = up[...] + up_in[...].astype(F32)
        grad_all = grad[...] + grad_in[...].astype(F32)
        sig = jax.nn.sigmoid(gate_all)
        gate_delta[...] = (grad_all * up_all * sig * (1.0 + gate_all * (1.0 - sig))).astype(BF16)
        up_delta[...] = (grad_all * gate_all * sig).astype(BF16)

    part = dot(gate_delta[...], masked(wg[...], mg[...]), NT)
    part = part + dot(up_delta[...], masked(wu[...], mu[...]), NT)
    put_blocks(part, blocks, half)


def input_grads(turn, sums, w_gate, w_up, keep_gate, keep_up, half):
    rows, width = sums[0].shape
    rows = rows // 2
    depth = w_gate.shape[0]
    feats = depth // half
    weight = pl.BlockSpec((feats, width), lambda i, s: (i ^ s[0], 0))
    keep = pl.BlockSpec((feats // BLK, 1, width), lambda i, s: (i ^ s[0], 0, 0))
    return call(
        functools.partial(input_grad_body, half),
        (half,),
        [whole(sums[0].shape)] * 6 + [weight, weight, keep, keep],
        [whole((rows, feats))] * (2 * half) + [whole(sums[0].shape)] * 2,
        [jax.ShapeDtypeStruct((rows, feats), BF16)] * (2 * half)
        + [jax.ShapeDtypeStruct(sums[0].shape, BF16)] * 2,
        [],
        8 * rows * depth * width,
        "input_grads",
    )(turn, *sums, w_gate, w_up, keep_gate, keep_up)


def weight_grad_body(turn_ref, tok, hid, gd, ud, cot, mg, mu, md, gg, ug, dg):
    tok_turned = tok[...].T
    for left, right, keep, out in (
        (tok_turned, gd, mg, gg),
        (tok_turned, ud, mu, ug),
        (hid[...].T, cot, md, dg),
    ):
        rows, cols = out.shape
        term = dot(left, right[...], NN).reshape(rows // BLK, BLK, cols) * keep[...]
        out[...] = term.reshape(rows, cols).astype(BF16)


def weight_grads(turn, tokens, hidden, gate_delta, up_delta, cotangent, keeps):
    rows, depth = tokens.shape
    width = hidden.shape[1]
    steps = max(depth, width) // 256
    deep, wide = depth // steps, width // steps
    if min(deep, wide) < BLK:
        steps = min(depth, width) // BLK
        deep, wide = depth // steps, width // steps
    by_depth = pl.BlockSpec((rows, deep), lambda i, s: (0, i))
    by_width = pl.BlockSpec((rows, wide), lambda i, s: (0, i))
    keep_deep = pl.BlockSpec((deep // BLK, 1, width), lambda i, s: (i, 0, 0))
    keep_wide = pl.BlockSpec((wide // BLK, 1, depth), lambda i, s: (i, 0, 0))
    return call(
        weight_grad_body,
        (steps,),
        [by_depth, by_width]
        + [whole((rows, width))] * 2
        + [whole((rows, depth)), keep_deep, keep_deep, keep_wide],
        [
            pl.BlockSpec((deep, width), lambda i, s: (i, 0)),
            pl.BlockSpec((deep, width), lambda i, s: (i, 0)),
            pl.BlockSpec((wide, depth), lambda i, s: (i, 0)),
        ],
        [
            jax.ShapeDtypeStruct((depth, width), BF16),
            jax.ShapeDtypeStruct((depth, width), BF16),
            jax.ShapeDtypeStruct((width, depth), BF16),
        ],
        [],
        6 * rows * depth * width,
        "weight_grads",
    )(turn, tokens, hidden, gate_delta, up_delta, cotangent, *keeps)


def expand_cols(block_mask):
    rows, cols = block_mask.shape
    grown = jnp.broadcast_to(block_mask[:, :, None], (rows, cols, BLK)).astype(F32)
    return grown.reshape(rows, 1, cols * BLK)


def routes(n):
    half = n // 2
    for k in range(n):
        yield [
            (t * 2 + core, ((((core ^ (k // half)) * half) + ((t % half) ^ (k % half))) * 2 + t // half))
            for t in range(n)
            for core in range(2)
        ]


def gather(block, n):
    return [lax.ppermute(block, ("tp", "dp"), route) for route in routes(n)]


def scatter(blocks, n):
    total = None
    for block, route in zip(blocks, routes(n)):
        got = lax.ppermute(block, ("tp", "dp"), [(b, a) for a, b in route]).astype(F32)
        total = got if total is None else total + got
    return total.astype(BF16)


def swap(part):
    return lax.ppermute(part, "dp", [(0, 1), (1, 0)])


def shards(tokens, cotangent, w_gate, w_up, w_down, gate_mask, up_mask, down_mask):
    n = lax.axis_size("tp")
    half = n // 2
    turn = (lax.axis_index("tp") % half).astype(jnp.int32).reshape(1)
    half_rows = w_gate.shape[0] // BLK
    offset = lax.axis_index("dp") * half_rows
    keep_gate = expand_cols(lax.dynamic_slice_in_dim(gate_mask, offset, half_rows, 0))
    keep_up = expand_cols(lax.dynamic_slice_in_dim(up_mask, offset, half_rows, 0))
    keep_down = expand_cols(lax.dynamic_slice_in_dim(down_mask, offset, half_rows, 1))

    tok_blocks = gather(tokens, n)
    tok_blocks, cotangent = lax.optimization_barrier((tok_blocks, cotangent))
    cot_blocks = gather(cotangent, n)
    gate, gate_out, up, up_out, tok = forward(
        turn, tok_blocks, w_gate, w_up, keep_gate, keep_up, half
    )
    gate_in, up_in = swap(gate_out), swap(up_out)
    grad, grad_out, cot = hidden_grads(turn, cot_blocks, w_down, keep_down, half)
    grad_in = swap(grad_out)
    *out_blocks, hidden = outputs(turn, gate, gate_in, up, up_in, w_down, keep_down, half)
    layer_out = scatter(out_blocks, n)
    *in_blocks, gate_delta, up_delta = input_grads(
        turn, (gate, gate_in, up, up_in, grad, grad_in), w_gate, w_up, keep_gate, keep_up, half
    )
    input_grad = scatter(in_blocks, n)
    gate_grad, up_grad, down_grad = weight_grads(
        turn, tok, hidden, gate_delta, up_delta, cot, (keep_gate, keep_up, keep_down)
    )
    return layer_out, input_grad, gate_grad, up_grad, down_grad


def solution(mesh):
    rows = P(("grp", "dp"), "tp")
    return jax.shard_map(
        shards,
        mesh=mesh,
        in_specs=(
            rows,
            rows,
            P("dp", "tp"),
            P("dp", "tp"),
            P("tp", "dp"),
            P(None, "tp"),
            P(None, "tp"),
            P("tp", None),
        ),
        out_specs=(rows, rows, rows, rows, P(("grp", "tp"), "dp")),
        check_vma=False,
    )
```

```python
import functools

import jax
import jax.numpy as jnp
from jax import lax
from jax.experimental import pallas as pl
from jax.experimental.pallas import tpu as pltpu
from jax.sharding import PartitionSpec as P

BLK = 128
BF16 = jnp.bfloat16
F32 = jnp.float32
NN = (((1,), (0,)), ((), ()))
NT = (((1,), (1,)), ((), ()))


def dot(left, right, dims):
    return lax.dot_general(left, right, dims, preferred_element_type=F32)


def masked(weight, keep):
    rows, cols = weight.shape
    kept = weight.reshape(rows // BLK, BLK, cols) * keep.astype(weight.dtype)
    return kept.reshape(rows, cols)


def whole(x):
    return pl.BlockSpec(x.shape, lambda i: (0,) * len(x.shape))


def in_hbm(x):
    return pltpu.with_memory_space_constraint(x, pltpu.HBM)


def call(body, sel, far, held, arrays, out_shape, scratch, flops, name, limit):
    return pl.pallas_call(
        body,
        grid=(1,),
        in_specs=[pl.BlockSpec(memory_space=pltpu.SMEM)]
        + [pl.BlockSpec(memory_space=pl.ANY)] * len(far)
        + [pl.BlockSpec(memory_space=pltpu.VMEM)] * len(held)
        + [whole(x) for x in arrays],
        out_specs=[whole(x) for x in out_shape],
        out_shape=out_shape,
        scratch_shapes=scratch,
        compiler_params=pltpu.CompilerParams(vmem_limit_bytes=limit * 1024 * 1024),
        cost_estimate=pl.CostEstimate(flops=flops, bytes_accessed=flops // 256, transcendentals=0),
        name=name,
    )(
        sel,
        *[in_hbm(x) for x in far],
        *[pltpu.with_memory_space_constraint(x, pltpu.VMEM) for x in held],
        *arrays,
    )


def prepare_body(weight, keep, out):
    rows = weight.shape[0]
    first = pl.multiple_of(pl.program_id(0) * rows, rows)
    out[pl.ds(first, rows), :] = masked(weight[...], keep[...])


def prepare(weight, keep, name):
    rows, cols = weight.shape
    tile = min(1024, rows)
    return pl.pallas_call(
        prepare_body,
        grid=(rows // tile,),
        in_specs=[
            pl.BlockSpec((tile, cols), lambda i: (i, 0)),
            pl.BlockSpec((tile // BLK, 1, cols), lambda i: (i, 0, 0)),
        ],
        out_specs=pl.BlockSpec(memory_space=pltpu.VMEM),
        out_shape=pltpu.VMEM((rows, cols), weight.dtype),
        compiler_params=pltpu.CompilerParams(vmem_limit_bytes=14 * 1024 * 1024),
        cost_estimate=pl.CostEstimate(flops=0, bytes_accessed=rows * cols // 16, transcendentals=0),
        name=name,
    )(in_hbm(weight), keep)


class Stream:
    def __init__(self, weights, buffers, sems, places):
        self.copies = []
        for c, (place, slot) in enumerate(places):
            for i, (weight, buffer) in enumerate(zip(weights, buffers)):
                self.copies.append(
                    pltpu.make_async_copy(weight.at[place], buffer.at[slot], sems.at[i, c])
                )
        for copy in self.copies:
            copy.start()
        self.step, self.count = 0, len(weights)

    def wait(self):
        for copy in self.copies[self.step : self.step + self.count]:
            copy.wait()
        self.step += self.count


def tiles(size, tile=512):
    tile = min(tile, size)
    return [slice(first, first + tile) for first in range(0, size, tile)]


def collect(pieces, refs, lhs, sel, half):
    feats = lhs.shape[1] // half
    for (block, near), ref in zip(pieces, refs):
        place = pl.ds(pl.multiple_of((block ^ sel[0]) * feats, feats), feats)

        def put(ref=ref, place=place):
            lhs[:, place] = ref[...]

        if near is None:
            put()
        else:
            pl.when(sel[1] == near)(put)


def shapes(rows, cols, *types):
    return [jax.ShapeDtypeStruct((rows, cols), kind) for kind in types]


def late(rows, cols):
    return [pltpu.HBM((rows, cols), BF16)]


def of_blocks(part):
    return slice(part.start // BLK, part.stop // BLK)


def forward_body(pieces, half, sel, wg, wu, mg, mu, *refs):
    blocks, refs = refs[: len(pieces)], refs[len(pieces) :]
    gate, up, lhs, wg_buf, wu_buf, sum_gate, sum_up, sems = refs
    deep = tiles(wg.shape[0])
    stream = Stream((wg, wu), (wg_buf, wu_buf), sems, [(rows, rows) for rows in deep])
    collect(pieces, blocks, lhs, sel, half)
    for step, rows in enumerate(deep):
        stream.wait()
        for buf, keep, total, out in ((wg_buf, mg, sum_gate, gate), (wu_buf, mu, sum_up, up)):
            for cols in tiles(out.shape[1]):
                weight = masked(buf[rows, cols], keep[of_blocks(rows), :, cols])
                part = dot(lhs[:, rows], weight, NN)
                if step > 0:
                    part = part + total[:, cols]
                if step < len(deep) - 1:
                    total[:, cols] = part
                else:
                    out[:, cols] = part.astype(BF16)


def forward(sel, got, w_gate, w_up, keep_gate, keep_up, half, rows):
    pieces, blocks = zip(*got)
    depth, width = w_gate.shape
    return call(
        functools.partial(forward_body, pieces, half),
        sel,
        [w_gate, w_up],
        [],
        [keep_gate, keep_up, *blocks],
        shapes(rows, width, BF16, BF16) + late(rows, depth),
        [pltpu.VMEM((depth, width), BF16)] * 2
        + [pltpu.VMEM((rows, width), F32)] * 2
        + [pltpu.SemaphoreType.DMA((2, 16))],
        rows * depth * width // 16,
        "forward",
        30,
    )


def middle_body(pieces, half, sel, weight, *refs):
    count = len(pieces)
    blocks, sums, refs = refs[:count], refs[count : count + 4], refs[count + 4 :]
    (grad, lhs, hidden, by_gate, by_up), outs = refs[:5], refs[5:]
    for cols in tiles(hidden.shape[1]):
        gate, up = add(sums[:2], cols), add(sums[2:], cols)
        sig = jax.nn.sigmoid(gate)
        silu = gate * sig
        hidden[:, cols] = (silu * up).astype(BF16)
        by_gate[:, cols] = up * sig * (1.0 + gate * (1.0 - sig))
        by_up[:, cols] = silu
    for out, place in zip(outs, places_of(range(half), sel, outs[0].shape[1])):
        out[...] = dot(hidden[...], weight[:, place], NN).astype(BF16)
    collect(pieces, blocks, lhs, sel, half)
    for cols in tiles(weight.shape[0]):
        grad[:, cols] = dot(lhs[...], weight[cols], NT).astype(BF16)


def middle(sel, got, sums, w_down, half, rows):
    pieces, blocks = zip(*got)
    width, depth = w_down.shape
    return call(
        functools.partial(middle_body, pieces, half),
        sel,
        [],
        [w_down],
        [*blocks, *sums],
        shapes(rows, width, BF16)
        + late(rows, depth)
        + late(rows, width)
        + shapes(rows, width, F32, F32)
        + late(rows, depth // half) * half,
        [],
        4 * rows * depth * width,
        "middle",
        20,
    )


def places_of(wanted, sel, feats):
    return [pl.ds(pl.multiple_of((j ^ sel[0]) * feats, feats), feats) for j in wanted]


def add(pair, cols):
    return pair[0][:, cols].astype(F32) + pair[1][:, cols].astype(F32)


def delta_tile(arrays, cols):
    by_gate, by_up, *grads = arrays
    grad = add(grads, cols)
    return (grad * by_gate[:, cols]).astype(BF16), (grad * by_up[:, cols]).astype(BF16)


def product_body(wanted, make, count, made, sel, *refs):
    sides = 2
    weights, refs = refs[:sides], refs[sides:]
    keeps, refs = refs[:sides], refs[sides:]
    arrays, refs = refs[:count], refs[count:]
    blocks, refs = refs[: len(wanted)], refs[len(wanted) :]
    lefts, refs = (refs[:made], refs[made:]) if make else (arrays, refs)
    buffers, sems = refs[:sides], refs[sides]
    feats = blocks[0].shape[1]
    kept = feats // BLK
    places = places_of(wanted, sel, feats)
    slots = [pl.ds(i * feats, feats) for i in range(len(wanted))]
    cut = lambda place: (place, slice(None))
    stream = Stream(weights, buffers, sems, [(cut(p), cut(q)) for p, q in zip(places, slots)])
    if make:
        for cols in tiles(lefts[0].shape[1]):
            for left, value in zip(lefts, make(arrays, cols)):
                left[:, cols] = value
    for j, place, slot, block in zip(wanted, places, slots, blocks):
        stream.wait()
        total = None
        for left, buffer, keep in zip(lefts, buffers, keeps):
            weight = masked(buffer[slot, :], keep[pl.ds((j ^ sel[0]) * kept, kept)])
            part = dot(left[...], weight, NT)
            total = part if total is None else total + part
        block[...] = total.astype(BF16)


def product(sel, wanted, make, arrays, weights, keeps, half, name):
    rows, width = arrays[0].shape
    depth = weights[0].size // width
    feats = depth // half
    made = len(weights) if make else 0
    held = len(wanted) * feats
    return call(
        functools.partial(product_body, wanted, make, len(arrays), made),
        sel,
        weights,
        [],
        [*keeps, *arrays],
        shapes(rows, feats, BF16) * len(wanted) + shapes(rows, width, BF16) * made,
        [pltpu.VMEM((held, width), BF16)] * 2 + [pltpu.SemaphoreType.DMA((2, len(wanted)))],
        2 * rows * held * width * len(weights),
        name,
        12 + len(weights) * held * width // 2**19,
    )


def weight_grad_body(left, right, keep, out):
    rows, cols = out.shape
    term = dot(left[...].T, right[...], NN).reshape(rows // BLK, BLK, cols) * keep[...]
    out[...] = term.reshape(rows, cols).astype(BF16)


def weight_grad(left, right, keep, name):
    rows, height = left.shape
    width = right.shape[1]
    tile = min(512, height)
    flops = 2 * rows * height * width
    return pl.pallas_call(
        weight_grad_body,
        grid=(height // tile,),
        in_specs=[
            pl.BlockSpec((rows, tile), lambda i: (0, i)),
            pl.BlockSpec((rows, width), lambda i: (0, 0)),
            pl.BlockSpec((tile // BLK, 1, width), lambda i: (i, 0, 0)),
        ],
        out_specs=pl.BlockSpec((tile, width), lambda i: (i, 0)),
        out_shape=jax.ShapeDtypeStruct((height, width), BF16),
        compiler_params=pltpu.CompilerParams(vmem_limit_bytes=16 * 1024 * 1024),
        cost_estimate=pl.CostEstimate(flops=flops, bytes_accessed=flops // 256, transcendentals=0),
        name=name,
    )(left, right, keep)


def expand_cols(block_mask):
    rows, cols = block_mask.shape
    grown = jnp.broadcast_to(block_mask[:, :, None], (rows, cols, BLK)).astype(F32)
    return grown.reshape(rows, 1, cols * BLK)


def permute(x, route):
    return lax.ppermute(x, ("tp", "dp"), route)


def back(route):
    return [(target, source) for source, target in route]


def swap(part):
    return lax.ppermute(part, "dp", [(0, 1), (1, 0)])


def direct_routes(n):
    half = n // 2
    for k in range(n):
        yield [
            (t * 2 + core, ((((core ^ (k // half)) * half) + ((t % half) ^ (k % half))) * 2 + t // half))
            for t in range(n)
            for core in range(2)
        ]


def direct_gather(block, n):
    half, rows = n // 2, block.shape[0]
    run = lax.axis_index("tp") // half
    got = [permute(block, route) for route in direct_routes(n)]
    pieces = []
    for j in range(half):
        both = jnp.where(
            run == 0,
            jnp.concatenate((got[j], got[half + j])),
            jnp.concatenate((got[half + j], got[j])),
        )
        pieces.append(((j, None), both))
    return pieces


def direct_scatter(blocks, n):
    half, rows = n // 2, blocks[0].shape[0] // 2
    run = lax.axis_index("tp") // half
    total = None
    for k, route in enumerate(direct_routes(n)):
        first = (run ^ (k // half)) * rows
        block = lax.dynamic_slice_in_dim(blocks[k % half], first, rows, 0)
        got = permute(block, back(route)).astype(F32)
        total = got if total is None else total + got
    return total.astype(BF16)


def staged_routes():
    names = ("near", "far", "across", "across_near", "across_far")
    pairs = {name: [] for name in names}
    for z in range(4):
        for y in range(2):
            for core in range(2):
                want = z // 2
                me = (z * 2 + y) * 2 + core
                at = lambda to_z, to_y, to_core: (to_z * 2 + to_y) * 2 + to_core
                pairs["near"].append((me, at(z ^ 1 if core == want else z ^ 3, y, want)))
                if core != want:
                    pairs["far"].append((me, at(z ^ 2, y, want)))
                pairs["across"].append((me, at(z, y ^ 1, core)))
                kind = "across_near" if core == want else "across_far"
                pairs[kind].append((me, at(z, y ^ 1, core)))
    return pairs


def after(x, *others):
    return lax.optimization_barrier((x, *others))[0]


def of_chip(block):
    other = swap(block)
    first = lax.axis_index("dp") == 0
    return jnp.concatenate((jnp.where(first, block, other), jnp.where(first, other, block)))


def staged_gathers(tokens, cotangent, near):
    routes = staged_routes()
    chip = of_chip(tokens)
    cot_chip = of_chip(after(cotangent, chip))
    one = permute(chip, routes["near"])
    two = permute(chip, routes["far"])
    beside = permute(chip, routes["across_near"])
    cot_one = permute(cot_chip, routes["near"])
    cot_here = jnp.where(near, cot_chip, permute(cot_chip, routes["far"]))
    one, two = after(one, cot_chip), after(two, cot_chip)
    tok_blocks = [
        ((0, 1), after(chip, cot_one, cot_here)),
        ((0, 0), two),
        ((2, None), one),
        ((1, 1), beside),
        ((3, None), permute(one, routes["across"])),
        ((1, 0), permute(two, routes["across_far"])),
    ]
    cot_blocks = [
        ((0, None), cot_here),
        ((2, None), cot_one),
        ((3, None), permute(cot_one, routes["across"])),
        ((1, None), permute(cot_here, routes["across"])),
    ]
    return tok_blocks, cot_blocks


def staged_across(blocks):
    across = staged_routes()["across"]
    return [permute(block, across) for block in blocks]


def staged_halves(blocks, got):
    return [
        (block.astype(F32) + other.astype(F32)).astype(BF16) for block, other in zip(blocks, got)
    ]


def staged_route(halves):
    routes = staged_routes()
    two, one = halves
    return permute(one, back(routes["near"])), permute(two, back(routes["far"]))


def staged_finish(halves, got, near):
    one, two = got
    total = one.astype(F32) + jnp.where(near, halves[0], two).astype(F32)
    rows = total.shape[0] // 2
    core = lax.axis_index("dp")
    theirs = lax.dynamic_slice_in_dim(total, (1 - core) * rows, rows, 0)
    mine = lax.dynamic_slice_in_dim(total, core * rows, rows, 0)
    return (mine + swap(theirs.astype(BF16)).astype(F32)).astype(BF16)


def shards(tokens, cotangent, w_gate, w_up, w_down, gate_mask, up_mask, down_mask):
    n = lax.axis_size("tp")
    half = n // 2
    rows = 2 * tokens.shape[0]
    at, core = lax.axis_index("tp"), lax.axis_index("dp")
    near = (at // half) == core
    sel = jnp.stack((at % half, near.astype(jnp.int32))).astype(jnp.int32)
    half_rows = w_gate.shape[0] // BLK
    offset = core * half_rows
    keep_gate = expand_cols(lax.dynamic_slice_in_dim(gate_mask, offset, half_rows, 0))
    keep_up = expand_cols(lax.dynamic_slice_in_dim(up_mask, offset, half_rows, 0))
    keep_down = expand_cols(lax.dynamic_slice_in_dim(down_mask, offset, half_rows, 1))

    staged = n == 8
    if staged:
        tok_blocks, cot_blocks = staged_gathers(tokens, cotangent, near)
    else:
        tok_blocks, cot_blocks = direct_gather(tokens, n), direct_gather(cotangent, n)
    gate, up, tok = forward(sel, tok_blocks, w_gate, w_up, keep_gate, keep_up, half, rows)
    late_up = after(up, *[block for _, block in cot_blocks[2:]]) if staged else up
    sums = [gate, swap(gate), up, swap(late_up)]
    w_held = prepare(w_down, after(keep_down, gate), "prepare_down")
    grad, cot, hidden, by_gate, by_up, *out_blocks = middle(
        sel, cot_blocks, sums, w_held, half, rows
    )
    deltas = [by_gate, by_up, grad, swap(grad)]
    gate_up = lambda wanted, make, arrays, name: product(
        sel, wanted, make, arrays, [w_gate, w_up], [keep_gate, keep_up], half, name
    )
    if staged:
        out_got = staged_across((out_blocks[1], out_blocks[3]))
        in_1, gate_delta, up_delta = gate_up((1,), delta_tile, deltas, "input_first")
        in_3, in_0, in_2 = gate_up((3, 0, 2), None, [gate_delta, up_delta], "input_rest")
        gate_grad = weight_grad(after(tok, in_0), gate_delta, keep_gate, "gate_grad")
        in_got = [after(x, gate_grad) for x in staged_across((in_1, in_3))]
        in_two = staged_halves((in_0,), in_got[:1])
        out_got = [after(x, *in_two) for x in out_got]
        out_halves = staged_halves((out_blocks[0], out_blocks[2]), out_got)
        up_grad = weight_grad(tok, after(up_delta, *out_halves), keep_up, "up_grad")
        in_halves = in_two + staged_halves((in_2,), [after(in_got[1], up_grad)])
        down_grad = weight_grad(hidden, after(cot, *in_halves), keep_down, "down_grad")
        layer_out = staged_finish(out_halves, staged_route(out_halves), near)
        input_grad = staged_finish(in_halves, staged_route(in_halves), near)
    else:
        *in_blocks, gate_delta, up_delta = gate_up(range(half), delta_tile, deltas, "input_grads")
        gate_grad = weight_grad(tok, gate_delta, keep_gate, "gate_grad")
        up_grad = weight_grad(tok, up_delta, keep_up, "up_grad")
        down_grad = weight_grad(hidden, cot, keep_down, "down_grad")
        layer_out, input_grad = direct_scatter(out_blocks, n), direct_scatter(in_blocks, n)
    return layer_out, input_grad, gate_grad, up_grad, down_grad


def solution(mesh):
    rows = P(("grp", "dp"), "tp")
    return jax.shard_map(
        shards,
        mesh=mesh,
        in_specs=(
            rows,
            rows,
            P("dp", "tp"),
            P("dp", "tp"),
            P("tp", "dp"),
            P(None, "tp"),
            P(None, "tp"),
            P("tp", None),
        ),
        out_specs=(rows, rows, rows, rows, P(("grp", "tp"), "dp")),
        check_vma=False,
    )
```

```python
import functools

import jax
import jax.numpy as jnp
from jax import lax
from jax.experimental import pallas as pl
from jax.experimental.pallas import tpu as pltpu
from jax.sharding import PartitionSpec as P

BLK = 128
BF16 = jnp.bfloat16
F32 = jnp.float32
NN = (((1,), (0,)), ((), ()))
NT = (((1,), (1,)), ((), ()))


def dot(left, right, dims):
    return lax.dot_general(left, right, dims, preferred_element_type=F32)


def masked(weight, keep):
    rows, cols = weight.shape
    kept = weight.reshape(rows // BLK, BLK, cols) * keep.astype(weight.dtype)
    return kept.reshape(rows, cols)


def whole(x):
    return pl.BlockSpec(x.shape, lambda i: (0,) * len(x.shape))


def in_hbm(x):
    return pltpu.with_memory_space_constraint(x, pltpu.HBM)


def call(body, sel, far, held, arrays, out_shape, scratch, flops, name, limit):
    return pl.pallas_call(
        body,
        grid=(1,),
        in_specs=[pl.BlockSpec(memory_space=pltpu.SMEM)]
        + [pl.BlockSpec(memory_space=pl.ANY)] * len(far)
        + [pl.BlockSpec(memory_space=pltpu.VMEM)] * len(held)
        + [whole(x) for x in arrays],
        out_specs=[whole(x) for x in out_shape],
        out_shape=out_shape,
        scratch_shapes=scratch,
        compiler_params=pltpu.CompilerParams(vmem_limit_bytes=limit * 1024 * 1024),
        cost_estimate=pl.CostEstimate(flops=flops, bytes_accessed=flops // 256, transcendentals=0),
        name=name,
    )(
        sel,
        *[in_hbm(x) for x in far],
        *[pltpu.with_memory_space_constraint(x, pltpu.VMEM) for x in held],
        *arrays,
    )


def prepare_body(weight, keep, out):
    rows = weight.shape[0]
    first = pl.multiple_of(pl.program_id(0) * rows, rows)
    out[pl.ds(first, rows), :] = masked(weight[...], keep[...])


def prepare(weight, keep, name):
    rows, cols = weight.shape
    tile = min(1024, rows)
    return pl.pallas_call(
        prepare_body,
        grid=(rows // tile,),
        in_specs=[
            pl.BlockSpec((tile, cols), lambda i: (i, 0)),
            pl.BlockSpec((tile // BLK, 1, cols), lambda i: (i, 0, 0)),
        ],
        out_specs=pl.BlockSpec(memory_space=pltpu.VMEM),
        out_shape=pltpu.VMEM((rows, cols), weight.dtype),
        compiler_params=pltpu.CompilerParams(vmem_limit_bytes=14 * 1024 * 1024),
        cost_estimate=pl.CostEstimate(flops=0, bytes_accessed=rows * cols // 16, transcendentals=0),
        name=name,
    )(in_hbm(weight), keep)


class Stream:
    def __init__(self, weights, buffers, sems, places):
        self.copies = []
        for c, (place, slot) in enumerate(places):
            for i, (weight, buffer) in enumerate(zip(weights, buffers)):
                self.copies.append(
                    pltpu.make_async_copy(weight.at[place], buffer.at[slot], sems.at[i, c])
                )
        for copy in self.copies:
            copy.start()
        self.step, self.count = 0, len(weights)

    def wait(self):
        for copy in self.copies[self.step : self.step + self.count]:
            copy.wait()
        self.step += self.count


def tiles(size, tile=512):
    tile = min(tile, size)
    return [slice(first, first + tile) for first in range(0, size, tile)]


def collect(pieces, refs, lhs, sel, half):
    feats = lhs.shape[1] // half
    for (block, near), ref in zip(pieces, refs):
        place = pl.ds(pl.multiple_of((block ^ sel[0]) * feats, feats), feats)

        def put(ref=ref, place=place):
            lhs[:, place] = ref[...]

        if near is None:
            put()
        else:
            pl.when(sel[1] == near)(put)


def shapes(rows, cols, *types):
    return [jax.ShapeDtypeStruct((rows, cols), kind) for kind in types]


def late(rows, cols):
    return [pltpu.HBM((rows, cols), BF16)]


def of_blocks(part):
    return slice(part.start // BLK, part.stop // BLK)


def forward_body(pieces, half, sel, wg, wu, mg, mu, *refs):
    blocks, refs = refs[: len(pieces)], refs[len(pieces) :]
    gate, up, lhs, wg_buf, wu_buf, sum_gate, sum_up, sems = refs
    deep = tiles(wg.shape[0])
    stream = Stream((wg, wu), (wg_buf, wu_buf), sems, [(rows, rows) for rows in deep])
    collect(pieces, blocks, lhs, sel, half)
    for step, rows in enumerate(deep):
        stream.wait()
        for buf, keep, total, out in ((wg_buf, mg, sum_gate, gate), (wu_buf, mu, sum_up, up)):
            for cols in tiles(out.shape[1]):
                weight = masked(buf[rows, cols], keep[of_blocks(rows), :, cols])
                part = dot(lhs[:, rows], weight, NN)
                if step > 0:
                    part = part + total[:, cols]
                if step < len(deep) - 1:
                    total[:, cols] = part
                else:
                    out[:, cols] = part.astype(BF16)


def forward(sel, got, w_gate, w_up, keep_gate, keep_up, half, rows):
    pieces, blocks = zip(*got)
    depth, width = w_gate.shape
    return call(
        functools.partial(forward_body, pieces, half),
        sel,
        [w_gate, w_up],
        [],
        [keep_gate, keep_up, *blocks],
        shapes(rows, width, BF16, BF16) + late(rows, depth),
        [pltpu.VMEM((depth, width), BF16)] * 2
        + [pltpu.VMEM((rows, width), F32)] * 2
        + [pltpu.SemaphoreType.DMA((2, 16))],
        rows * depth * width // 16,
        "forward",
        30,
    )


def middle_body(pieces, half, sel, weight, *refs):
    count = len(pieces)
    blocks, sums, refs = refs[:count], refs[count : count + 4], refs[count + 4 :]
    (grad, lhs, hidden, by_gate, by_up), outs = refs[:5], refs[5:]
    for cols in tiles(hidden.shape[1]):
        gate, up = add(sums[:2], cols), add(sums[2:], cols)
        sig = jax.nn.sigmoid(gate)
        silu = gate * sig
        hidden[:, cols] = (silu * up).astype(BF16)
        by_gate[:, cols] = up * sig * (1.0 + gate * (1.0 - sig))
        by_up[:, cols] = silu
    for out, place in zip(outs, places_of(range(half), sel, outs[0].shape[1])):
        out[...] = dot(hidden[...], weight[:, place], NN).astype(BF16)
    collect(pieces, blocks, lhs, sel, half)
    for cols in tiles(weight.shape[0]):
        grad[:, cols] = dot(lhs[...], weight[cols], NT).astype(BF16)


def middle(sel, got, sums, w_down, half, rows):
    pieces, blocks = zip(*got)
    width, depth = w_down.shape
    return call(
        functools.partial(middle_body, pieces, half),
        sel,
        [],
        [w_down],
        [*[in_hbm(block) for block in blocks], *sums],
        shapes(rows, width, BF16)
        + late(rows, depth)
        + late(rows, width)
        + shapes(rows, width, F32)
        + [pltpu.HBM((rows, width), F32)]
        + late(rows, depth // half) * half,
        [],
        4 * rows * depth * width,
        "middle",
        20,
    )


def places_of(wanted, sel, feats):
    return [pl.ds(pl.multiple_of((j ^ sel[0]) * feats, feats), feats) for j in wanted]


def add(pair, cols):
    return pair[0][:, cols].astype(F32) + pair[1][:, cols].astype(F32)


def delta_tile(arrays, cols):
    by_gate, by_up, *grads = arrays
    grad = add(grads, cols)
    return (grad * by_gate[:, cols]).astype(BF16), (grad * by_up[:, cols]).astype(BF16)


def product_body(wanted, make, count, made, sel, *refs):
    sides = 2
    weights, refs = refs[:sides], refs[sides:]
    keeps, refs = refs[:sides], refs[sides:]
    arrays, refs = refs[:count], refs[count:]
    blocks, refs = refs[: len(wanted)], refs[len(wanted) :]
    lefts, refs = (refs[:made], refs[made:]) if make else (arrays, refs)
    buffers, sems = refs[:sides], refs[sides]
    feats = blocks[0].shape[1]
    kept = feats // BLK
    places = places_of(wanted, sel, feats)
    slots = [pl.ds(i * feats, feats) for i in range(len(wanted))]
    cut = lambda place: (place, slice(None))
    stream = Stream(weights, buffers, sems, [(cut(p), cut(q)) for p, q in zip(places, slots)])
    if make:
        for cols in tiles(lefts[0].shape[1]):
            for left, value in zip(lefts, make(arrays, cols)):
                left[:, cols] = value
    for j, place, slot, block in zip(wanted, places, slots, blocks):
        stream.wait()
        total = None
        for left, buffer, keep in zip(lefts, buffers, keeps):
            weight = masked(buffer[slot, :], keep[pl.ds((j ^ sel[0]) * kept, kept)])
            part = dot(left[...], weight, NT)
            total = part if total is None else total + part
        block[...] = total.astype(BF16)


def product(sel, wanted, make, arrays, weights, keeps, half, name):
    rows, width = arrays[0].shape
    depth = weights[0].size // width
    feats = depth // half
    made = len(weights) if make else 0
    held = len(wanted) * feats
    return call(
        functools.partial(product_body, wanted, make, len(arrays), made),
        sel,
        weights,
        [],
        [*keeps, *arrays],
        shapes(rows, feats, BF16) * len(wanted) + shapes(rows, width, BF16) * made,
        [pltpu.VMEM((held, width), BF16)] * 2 + [pltpu.SemaphoreType.DMA((2, len(wanted)))],
        2 * rows * held * width * len(weights),
        name,
        12 + len(weights) * held * width // 2**19,
    )


def weight_grad_body(left, right, keep, out):
    rows, cols = out.shape
    term = dot(left[...].T, right[...], NN).reshape(rows // BLK, BLK, cols) * keep[...]
    out[...] = term.reshape(rows, cols).astype(BF16)


def weight_grad(left, right, keep, name):
    rows, height = left.shape
    width = right.shape[1]
    tile = min(512, height)
    flops = 2 * rows * height * width
    return pl.pallas_call(
        weight_grad_body,
        grid=(height // tile,),
        in_specs=[
            pl.BlockSpec((rows, tile), lambda i: (0, i)),
            pl.BlockSpec((rows, width), lambda i: (0, 0)),
            pl.BlockSpec((tile // BLK, 1, width), lambda i: (i, 0, 0)),
        ],
        out_specs=pl.BlockSpec((tile, width), lambda i: (i, 0)),
        out_shape=jax.ShapeDtypeStruct((height, width), BF16),
        compiler_params=pltpu.CompilerParams(vmem_limit_bytes=16 * 1024 * 1024),
        cost_estimate=pl.CostEstimate(flops=flops, bytes_accessed=flops // 256, transcendentals=0),
        name=name,
    )(left, right, keep)


def expand_cols(block_mask):
    rows, cols = block_mask.shape
    grown = jnp.broadcast_to(block_mask[:, :, None], (rows, cols, BLK)).astype(F32)
    return grown.reshape(rows, 1, cols * BLK)


def permute(x, route):
    return lax.ppermute(x, ("tp", "dp"), route)


def back(route):
    return [(target, source) for source, target in route]


def swap(part):
    return lax.ppermute(part, "dp", [(0, 1), (1, 0)])


def direct_routes(n):
    half = n // 2
    for k in range(n):
        yield [
            (t * 2 + core, ((((core ^ (k // half)) * half) + ((t % half) ^ (k % half))) * 2 + t // half))
            for t in range(n)
            for core in range(2)
        ]


def direct_gather(block, n):
    half, rows = n // 2, block.shape[0]
    run = lax.axis_index("tp") // half
    got = [permute(block, route) for route in direct_routes(n)]
    pieces = []
    for j in range(half):
        both = jnp.where(
            run == 0,
            jnp.concatenate((got[j], got[half + j])),
            jnp.concatenate((got[half + j], got[j])),
        )
        pieces.append(((j, None), both))
    return pieces


def direct_scatter(blocks, n):
    half, rows = n // 2, blocks[0].shape[0] // 2
    run = lax.axis_index("tp") // half
    total = None
    for k, route in enumerate(direct_routes(n)):
        first = (run ^ (k // half)) * rows
        block = lax.dynamic_slice_in_dim(blocks[k % half], first, rows, 0)
        got = permute(block, back(route)).astype(F32)
        total = got if total is None else total + got
    return total.astype(BF16)


def staged_routes():
    names = ("near", "far", "across", "across_near", "across_far")
    pairs = {name: [] for name in names}
    for z in range(4):
        for y in range(2):
            for core in range(2):
                want = z // 2
                me = (z * 2 + y) * 2 + core
                at = lambda to_z, to_y, to_core: (to_z * 2 + to_y) * 2 + to_core
                pairs["near"].append((me, at(z ^ 1 if core == want else z ^ 3, y, want)))
                if core != want:
                    pairs["far"].append((me, at(z ^ 2, y, want)))
                pairs["across"].append((me, at(z, y ^ 1, core)))
                kind = "across_near" if core == want else "across_far"
                pairs[kind].append((me, at(z, y ^ 1, core)))
    return pairs


def after(x, *others):
    return lax.optimization_barrier((x, *others))[0]


def of_chip(block):
    other = swap(block)
    first = lax.axis_index("dp") == 0
    return jnp.concatenate((jnp.where(first, block, other), jnp.where(first, other, block)))


def staged_gathers(tokens, cotangent, near):
    routes = staged_routes()
    chip = of_chip(tokens)
    cot_chip = of_chip(after(cotangent, chip))
    one = permute(chip, routes["near"])
    two = permute(chip, routes["far"])
    beside = permute(chip, routes["across_near"])
    cot_one = permute(cot_chip, routes["near"])
    cot_here = jnp.where(near, cot_chip, permute(cot_chip, routes["far"]))
    one, two = after(one, cot_chip), after(two, cot_chip)
    tok_blocks = [
        ((0, 1), after(chip, cot_one, cot_here)),
        ((0, 0), two),
        ((2, None), one),
        ((1, 1), beside),
        ((3, None), permute(one, routes["across"])),
        ((1, 0), permute(two, routes["across_far"])),
    ]
    cot_blocks = [
        ((0, None), cot_here),
        ((2, None), cot_one),
        ((3, None), permute(cot_one, routes["across"])),
        ((1, None), permute(cot_here, routes["across"])),
    ]
    return tok_blocks, cot_blocks


def staged_across(blocks):
    across = staged_routes()["across"]
    return [permute(block, across) for block in blocks]


def staged_halves(blocks, got):
    return [
        (block.astype(F32) + other.astype(F32)).astype(BF16) for block, other in zip(blocks, got)
    ]


def staged_route(halves):
    routes = staged_routes()
    two, one = halves
    return permute(one, back(routes["near"])), permute(two, back(routes["far"]))


def staged_finish(halves, got, near):
    one, two = got
    total = one.astype(F32) + jnp.where(near, halves[0], two).astype(F32)
    rows = total.shape[0] // 2
    core = lax.axis_index("dp")
    theirs = lax.dynamic_slice_in_dim(total, (1 - core) * rows, rows, 0)
    mine = lax.dynamic_slice_in_dim(total, core * rows, rows, 0)
    return (mine + swap(theirs.astype(BF16)).astype(F32)).astype(BF16)


def shards(tokens, cotangent, w_gate, w_up, w_down, gate_mask, up_mask, down_mask):
    n = lax.axis_size("tp")
    half = n // 2
    rows = 2 * tokens.shape[0]
    at, core = lax.axis_index("tp"), lax.axis_index("dp")
    near = (at // half) == core
    sel = jnp.stack((at % half, near.astype(jnp.int32))).astype(jnp.int32)
    half_rows = w_gate.shape[0] // BLK
    offset = core * half_rows
    keep_gate = expand_cols(lax.dynamic_slice_in_dim(gate_mask, offset, half_rows, 0))
    keep_up = expand_cols(lax.dynamic_slice_in_dim(up_mask, offset, half_rows, 0))
    keep_down = expand_cols(lax.dynamic_slice_in_dim(down_mask, offset, half_rows, 1))

    staged = n == 8
    if staged:
        tok_blocks, cot_blocks = staged_gathers(tokens, cotangent, near)
    else:
        tok_blocks, cot_blocks = direct_gather(tokens, n), direct_gather(cotangent, n)
    gate, up, tok = forward(sel, tok_blocks, w_gate, w_up, keep_gate, keep_up, half, rows)
    late_up = after(up, *[block for _, block in cot_blocks[2:]]) if staged else up
    sums = [gate, swap(gate), up, swap(late_up)]
    w_held = prepare(w_down, after(keep_down, gate), "prepare_down")
    grad, cot, hidden, by_gate, by_up, *out_blocks = middle(
        sel, cot_blocks, sums, w_held, half, rows
    )
    deltas = [by_gate, in_hbm(by_up), grad, swap(grad)]
    gate_up = lambda wanted, make, arrays, name: product(
        sel, wanted, make, arrays, [w_gate, w_up], [keep_gate, keep_up], half, name
    )
    if staged:
        out_got = staged_across((out_blocks[1], out_blocks[3]))
        in_1, gate_delta, up_delta = gate_up((1,), delta_tile, deltas, "input_first")
        in_3, in_0, in_2 = gate_up((3, 0, 2), None, [gate_delta, up_delta], "input_rest")
        gate_grad = weight_grad(after(tok, in_0), gate_delta, keep_gate, "gate_grad")
        in_got = [after(x, gate_grad) for x in staged_across((in_1, in_3))]
        in_two = staged_halves((in_0,), in_got[:1])
        out_got = [after(x, *in_two) for x in out_got]
        out_halves = staged_halves((out_blocks[0], out_blocks[2]), out_got)
        up_grad = weight_grad(tok, after(up_delta, *out_halves), keep_up, "up_grad")
        in_halves = in_two + staged_halves((in_2,), [after(in_got[1], up_grad)])
        down_grad = weight_grad(hidden, after(cot, *in_halves), keep_down, "down_grad")
        layer_out = staged_finish(out_halves, staged_route(out_halves), near)
        input_grad = staged_finish(in_halves, staged_route(in_halves), near)
    else:
        *in_blocks, gate_delta, up_delta = gate_up(range(half), delta_tile, deltas, "input_grads")
        gate_grad = weight_grad(tok, gate_delta, keep_gate, "gate_grad")
        up_grad = weight_grad(tok, up_delta, keep_up, "up_grad")
        down_grad = weight_grad(hidden, cot, keep_down, "down_grad")
        layer_out, input_grad = direct_scatter(out_blocks, n), direct_scatter(in_blocks, n)
    return layer_out, input_grad, gate_grad, up_grad, down_grad


def solution(mesh):
    rows = P(("grp", "dp"), "tp")
    return jax.shard_map(
        shards,
        mesh=mesh,
        in_specs=(
            rows,
            rows,
            P("dp", "tp"),
            P("dp", "tp"),
            P("tp", "dp"),
            P(None, "tp"),
            P(None, "tp"),
            P("tp", None),
        ),
        out_specs=(rows, rows, rows, rows, P(("grp", "tp"), "dp")),
        check_vma=False,
    )
```

```python
import functools

import jax
import jax.numpy as jnp
from jax import lax
from jax.experimental import pallas as pl
from jax.experimental.pallas import tpu as pltpu
from jax.sharding import PartitionSpec as P

BLK = 128
BF16 = jnp.bfloat16
F32 = jnp.float32
NN = (((1,), (0,)), ((), ()))
NT = (((1,), (1,)), ((), ()))


def dot(left, right, dims):
    return lax.dot_general(left, right, dims, preferred_element_type=F32)


def masked(weight, keep):
    rows, cols = weight.shape
    kept = weight.reshape(rows // BLK, BLK, cols) * keep.astype(weight.dtype)
    return kept.reshape(rows, cols)


def whole(x):
    return pl.BlockSpec(x.shape, lambda i: (0,) * len(x.shape))


def in_hbm(x):
    return pltpu.with_memory_space_constraint(x, pltpu.HBM)


def call(body, sel, far, held, arrays, out_shape, scratch, flops, name, limit):
    return pl.pallas_call(
        body,
        grid=(1,),
        in_specs=[pl.BlockSpec(memory_space=pltpu.SMEM)]
        + [pl.BlockSpec(memory_space=pl.ANY)] * len(far)
        + [pl.BlockSpec(memory_space=pltpu.VMEM)] * len(held)
        + [whole(x) for x in arrays],
        out_specs=[whole(x) for x in out_shape],
        out_shape=out_shape,
        scratch_shapes=scratch,
        compiler_params=pltpu.CompilerParams(vmem_limit_bytes=limit * 1024 * 1024),
        cost_estimate=pl.CostEstimate(flops=flops, bytes_accessed=flops // 256, transcendentals=0),
        name=name,
    )(
        sel,
        *[in_hbm(x) for x in far],
        *[pltpu.with_memory_space_constraint(x, pltpu.VMEM) for x in held],
        *arrays,
    )


def prepare_body(weight, keep, out):
    rows = weight.shape[0]
    first = pl.multiple_of(pl.program_id(0) * rows, rows)
    out[pl.ds(first, rows), :] = masked(weight[...], keep[...])


def prepare(weight, keep, name):
    rows, cols = weight.shape
    tile = min(1024, rows)
    return pl.pallas_call(
        prepare_body,
        grid=(rows // tile,),
        in_specs=[
            pl.BlockSpec((tile, cols), lambda i: (i, 0)),
            pl.BlockSpec((tile // BLK, 1, cols), lambda i: (i, 0, 0)),
        ],
        out_specs=pl.BlockSpec(memory_space=pltpu.VMEM),
        out_shape=pltpu.VMEM((rows, cols), weight.dtype),
        compiler_params=pltpu.CompilerParams(vmem_limit_bytes=14 * 1024 * 1024),
        cost_estimate=pl.CostEstimate(flops=0, bytes_accessed=rows * cols // 16, transcendentals=0),
        name=name,
    )(in_hbm(weight), keep)


class Stream:
    def __init__(self, weights, buffers, sems, places):
        self.copies = []
        for c, (place, slot) in enumerate(places):
            for i, (weight, buffer) in enumerate(zip(weights, buffers)):
                self.copies.append(
                    pltpu.make_async_copy(weight.at[place], buffer.at[slot], sems.at[i, c])
                )
        for copy in self.copies:
            copy.start()
        self.step, self.count = 0, len(weights)

    def wait(self):
        for copy in self.copies[self.step : self.step + self.count]:
            copy.wait()
        self.step += self.count


def tiles(size, tile=512):
    tile = min(tile, size)
    return [slice(first, first + tile) for first in range(0, size, tile)]


def collect(pieces, refs, lhs, sel, half):
    feats = lhs.shape[1] // half
    for (block, near), ref in zip(pieces, refs):
        place = pl.ds(pl.multiple_of((block ^ sel[0]) * feats, feats), feats)

        def put(ref=ref, place=place):
            lhs[:, place] = ref[...]

        if near is None:
            put()
        else:
            pl.when(sel[1] == near)(put)


def shapes(rows, cols, *types):
    return [jax.ShapeDtypeStruct((rows, cols), kind) for kind in types]


def late(rows, cols):
    return [pltpu.HBM((rows, cols), BF16)]


def of_blocks(part):
    return slice(part.start // BLK, part.stop // BLK)


def forward_body(pieces, half, sel, wg, wu, mg, mu, *refs):
    blocks, refs = refs[: len(pieces)], refs[len(pieces) :]
    gate, up, lhs, wg_buf, wu_buf, sum_gate, sum_up, sems = refs
    deep = tiles(wg.shape[0])
    stream = Stream((wg, wu), (wg_buf, wu_buf), sems, [(rows, rows) for rows in deep])
    collect(pieces, blocks, lhs, sel, half)
    for step, rows in enumerate(deep):
        stream.wait()
        for buf, keep, total, out in ((wg_buf, mg, sum_gate, gate), (wu_buf, mu, sum_up, up)):
            for cols in tiles(out.shape[1]):
                weight = masked(buf[rows, cols], keep[of_blocks(rows), :, cols])
                part = dot(lhs[:, rows], weight, NN)
                if step > 0:
                    part = part + total[:, cols]
                if step < len(deep) - 1:
                    total[:, cols] = part
                else:
                    out[:, cols] = part.astype(BF16)


def forward(sel, got, w_gate, w_up, keep_gate, keep_up, half, rows):
    pieces, blocks = zip(*got)
    depth, width = w_gate.shape
    return call(
        functools.partial(forward_body, pieces, half),
        sel,
        [w_gate, w_up],
        [],
        [keep_gate, keep_up, *blocks],
        shapes(rows, width, BF16, BF16) + late(rows, depth),
        [pltpu.VMEM((depth, width), BF16)] * 2
        + [pltpu.VMEM((rows, width), F32)] * 2
        + [pltpu.SemaphoreType.DMA((2, 16))],
        rows * depth * width // 16,
        "forward",
        30,
    )


def middle_body(pieces, half, sel, weight, *refs):
    count = len(pieces)
    blocks, sums, refs = refs[:count], refs[count : count + 4], refs[count + 4 :]
    (grad, lhs, hidden, by_gate, by_up), outs = refs[:5], refs[5:]
    for cols in tiles(hidden.shape[1]):
        gate, up = add(sums[:2], cols), add(sums[2:], cols)
        sig = jax.nn.sigmoid(gate)
        silu = gate * sig
        hidden[:, cols] = (silu * up).astype(BF16)
        by_gate[:, cols] = up * sig * (1.0 + gate * (1.0 - sig))
        by_up[:, cols] = silu
    for out, place in zip(outs, places_of(range(half), sel, outs[0].shape[1])):
        out[...] = dot(hidden[...], weight[:, place], NN).astype(BF16)
    collect(pieces, blocks, lhs, sel, half)
    for cols in tiles(weight.shape[0]):
        grad[:, cols] = dot(lhs[...], weight[cols], NT).astype(BF16)


def middle(sel, got, sums, w_down, half, rows):
    pieces, blocks = zip(*got)
    width, depth = w_down.shape
    return call(
        functools.partial(middle_body, pieces, half),
        sel,
        [],
        [w_down],
        [*[in_hbm(block) for block in blocks], *sums],
        shapes(rows, width, BF16)
        + late(rows, depth)
        + late(rows, width)
        + shapes(rows, width, F32)
        + [pltpu.HBM((rows, width), F32)]
        + late(rows, depth // half) * half,
        [],
        4 * rows * depth * width,
        "middle",
        20,
    )


def places_of(wanted, sel, feats):
    return [pl.ds(pl.multiple_of((j ^ sel[0]) * feats, feats), feats) for j in wanted]


def add(pair, cols):
    return pair[0][:, cols].astype(F32) + pair[1][:, cols].astype(F32)


def delta_tile(arrays, cols):
    by_gate, by_up, *grads = arrays
    grad = add(grads, cols)
    return (grad * by_gate[:, cols]).astype(BF16), (grad * by_up[:, cols]).astype(BF16)


def product_body(wanted, make, count, made, sel, *refs):
    sides = 2
    weights, refs = refs[:sides], refs[sides:]
    keeps, refs = refs[:sides], refs[sides:]
    arrays, refs = refs[:count], refs[count:]
    blocks, refs = refs[: len(wanted)], refs[len(wanted) :]
    lefts, refs = (refs[:made], refs[made:]) if make else (arrays, refs)
    buffers, sems = refs[:sides], refs[sides]
    feats = blocks[0].shape[1]
    kept = feats // BLK
    places = places_of(wanted, sel, feats)
    slots = [pl.ds(i * feats, feats) for i in range(len(wanted))]
    cut = lambda place: (place, slice(None))
    stream = Stream(weights, buffers, sems, [(cut(p), cut(q)) for p, q in zip(places, slots)])
    if make:
        for cols in tiles(lefts[0].shape[1]):
            for left, value in zip(lefts, make(arrays, cols)):
                left[:, cols] = value
    for j, place, slot, block in zip(wanted, places, slots, blocks):
        stream.wait()
        total = None
        for left, buffer, keep in zip(lefts, buffers, keeps):
            weight = masked(buffer[slot, :], keep[pl.ds((j ^ sel[0]) * kept, kept)])
            part = dot(left[...], weight, NT)
            total = part if total is None else total + part
        block[...] = total.astype(BF16)


def product(sel, wanted, make, arrays, weights, keeps, half, name):
    rows, width = arrays[0].shape
    depth = weights[0].size // width
    feats = depth // half
    made = len(weights) if make else 0
    held = len(wanted) * feats
    return call(
        functools.partial(product_body, wanted, make, len(arrays), made),
        sel,
        weights,
        [],
        [*keeps, *arrays],
        shapes(rows, feats, BF16) * len(wanted) + shapes(rows, width, BF16) * made,
        [pltpu.VMEM((held, width), BF16)] * 2 + [pltpu.SemaphoreType.DMA((2, len(wanted)))],
        2 * rows * held * width * len(weights),
        name,
        12 + len(weights) * held * width // 2**19,
    )


def weight_grad_body(left, right, keep, out):
    rows, cols = out.shape
    term = dot(left[...].T, right[...], NN).reshape(rows // BLK, BLK, cols) * keep[...]
    out[...] = term.reshape(rows, cols).astype(BF16)


def weight_grad(left, right, keep, name):
    rows, height = left.shape
    width = right.shape[1]
    tile = min(1024, height)
    flops = 2 * rows * height * width
    return pl.pallas_call(
        weight_grad_body,
        grid=(height // tile,),
        in_specs=[
            pl.BlockSpec((rows, tile), lambda i: (0, i)),
            pl.BlockSpec((rows, width), lambda i: (0, 0)),
            pl.BlockSpec((tile // BLK, 1, width), lambda i: (i, 0, 0)),
        ],
        out_specs=pl.BlockSpec((tile, width), lambda i: (i, 0)),
        out_shape=jax.ShapeDtypeStruct((height, width), BF16),
        compiler_params=pltpu.CompilerParams(vmem_limit_bytes=28 * 1024 * 1024),
        cost_estimate=pl.CostEstimate(flops=flops, bytes_accessed=flops // 256, transcendentals=0),
        name=name,
    )(left, right, keep)


def expand_cols(block_mask):
    rows, cols = block_mask.shape
    grown = jnp.broadcast_to(block_mask[:, :, None], (rows, cols, BLK)).astype(F32)
    return grown.reshape(rows, 1, cols * BLK)


def permute(x, route):
    return lax.ppermute(x, ("tp", "dp"), route)


def back(route):
    return [(target, source) for source, target in route]


def swap(part):
    return lax.ppermute(part, "dp", [(0, 1), (1, 0)])


def direct_routes(n):
    half = n // 2
    for k in range(n):
        yield [
            (t * 2 + core, ((((core ^ (k // half)) * half) + ((t % half) ^ (k % half))) * 2 + t // half))
            for t in range(n)
            for core in range(2)
        ]


def direct_gather(block, n):
    half, rows = n // 2, block.shape[0]
    run = lax.axis_index("tp") // half
    got = [permute(block, route) for route in direct_routes(n)]
    pieces = []
    for j in range(half):
        both = jnp.where(
            run == 0,
            jnp.concatenate((got[j], got[half + j])),
            jnp.concatenate((got[half + j], got[j])),
        )
        pieces.append(((j, None), both))
    return pieces


def direct_scatter(blocks, n):
    half, rows = n // 2, blocks[0].shape[0] // 2
    run = lax.axis_index("tp") // half
    total = None
    for k, route in enumerate(direct_routes(n)):
        first = (run ^ (k // half)) * rows
        block = lax.dynamic_slice_in_dim(blocks[k % half], first, rows, 0)
        got = permute(block, back(route)).astype(F32)
        total = got if total is None else total + got
    return total.astype(BF16)


def staged_routes():
    names = ("near", "far", "across", "across_near", "across_far")
    pairs = {name: [] for name in names}
    for z in range(4):
        for y in range(2):
            for core in range(2):
                want = z // 2
                me = (z * 2 + y) * 2 + core
                at = lambda to_z, to_y, to_core: (to_z * 2 + to_y) * 2 + to_core
                pairs["near"].append((me, at(z ^ 1 if core == want else z ^ 3, y, want)))
                if core != want:
                    pairs["far"].append((me, at(z ^ 2, y, want)))
                pairs["across"].append((me, at(z, y ^ 1, core)))
                kind = "across_near" if core == want else "across_far"
                pairs[kind].append((me, at(z, y ^ 1, core)))
    return pairs


def after(x, *others):
    return lax.optimization_barrier((x, *others))[0]


def of_chip(block):
    other = swap(block)
    first = lax.axis_index("dp") == 0
    return jnp.concatenate((jnp.where(first, block, other), jnp.where(first, other, block)))


def staged_gathers(tokens, cotangent, near):
    routes = staged_routes()
    chip = of_chip(tokens)
    cot_chip = of_chip(after(cotangent, chip))
    one = permute(chip, routes["near"])
    two = permute(chip, routes["far"])
    beside = permute(chip, routes["across_near"])
    cot_one = permute(cot_chip, routes["near"])
    cot_here = jnp.where(near, cot_chip, permute(cot_chip, routes["far"]))
    one, two = after(one, cot_chip), after(two, cot_chip)
    tok_blocks = [
        ((0, 1), after(chip, cot_one, cot_here)),
        ((0, 0), two),
        ((2, None), one),
        ((1, 1), beside),
        ((3, None), permute(one, routes["across"])),
        ((1, 0), permute(two, routes["across_far"])),
    ]
    cot_blocks = [
        ((0, None), cot_here),
        ((2, None), cot_one),
        ((3, None), permute(cot_one, routes["across"])),
        ((1, None), permute(cot_here, routes["across"])),
    ]
    return tok_blocks, cot_blocks


def staged_across(blocks):
    across = staged_routes()["across"]
    return [permute(block, across) for block in blocks]


def staged_halves(blocks, got):
    return [
        (block.astype(F32) + other.astype(F32)).astype(BF16) for block, other in zip(blocks, got)
    ]


def staged_route(halves):
    routes = staged_routes()
    two, one = halves
    return permute(one, back(routes["near"])), permute(two, back(routes["far"]))


def staged_finish(halves, got, near):
    one, two = got
    total = one.astype(F32) + jnp.where(near, halves[0], two).astype(F32)
    rows = total.shape[0] // 2
    core = lax.axis_index("dp")
    theirs = lax.dynamic_slice_in_dim(total, (1 - core) * rows, rows, 0)
    mine = lax.dynamic_slice_in_dim(total, core * rows, rows, 0)
    return (mine + swap(theirs.astype(BF16)).astype(F32)).astype(BF16)


def shards(tokens, cotangent, w_gate, w_up, w_down, gate_mask, up_mask, down_mask):
    n = lax.axis_size("tp")
    half = n // 2
    rows = 2 * tokens.shape[0]
    at, core = lax.axis_index("tp"), lax.axis_index("dp")
    near = (at // half) == core
    sel = jnp.stack((at % half, near.astype(jnp.int32))).astype(jnp.int32)
    half_rows = w_gate.shape[0] // BLK
    offset = core * half_rows
    keep_gate = expand_cols(lax.dynamic_slice_in_dim(gate_mask, offset, half_rows, 0))
    keep_up = expand_cols(lax.dynamic_slice_in_dim(up_mask, offset, half_rows, 0))
    keep_down = expand_cols(lax.dynamic_slice_in_dim(down_mask, offset, half_rows, 1))

    staged = n == 8
    if staged:
        tok_blocks, cot_blocks = staged_gathers(tokens, cotangent, near)
    else:
        tok_blocks, cot_blocks = direct_gather(tokens, n), direct_gather(cotangent, n)
    gate, up, tok = forward(sel, tok_blocks, w_gate, w_up, keep_gate, keep_up, half, rows)
    late_up = after(up, *[block for _, block in cot_blocks[2:]]) if staged else up
    sums = [gate, swap(gate), up, swap(late_up)]
    w_held = prepare(w_down, after(keep_down, gate), "prepare_down")
    grad, cot, hidden, by_gate, by_up, *out_blocks = middle(
        sel, cot_blocks, sums, w_held, half, rows
    )
    deltas = [by_gate, in_hbm(by_up), grad, swap(grad)]
    gate_up = lambda wanted, make, arrays, name: product(
        sel, wanted, make, arrays, [w_gate, w_up], [keep_gate, keep_up], half, name
    )
    if staged:
        out_got = staged_across((out_blocks[1], out_blocks[3]))
        in_1, gate_delta, up_delta = gate_up((1,), delta_tile, deltas, "input_first")
        in_3, in_0, in_2 = gate_up((3, 0, 2), None, [gate_delta, up_delta], "input_rest")
        gate_grad = weight_grad(after(tok, in_0), gate_delta, keep_gate, "gate_grad")
        in_got = [after(x, gate_grad) for x in staged_across((in_1, in_3))]
        in_two = staged_halves((in_0,), in_got[:1])
        out_got = [after(x, *in_two) for x in out_got]
        out_halves = staged_halves((out_blocks[0], out_blocks[2]), out_got)
        up_grad = weight_grad(tok, after(up_delta, *out_halves), keep_up, "up_grad")
        in_halves = in_two + staged_halves((in_2,), [after(in_got[1], up_grad)])
        down_grad = weight_grad(hidden, after(cot, *in_halves), keep_down, "down_grad")
        layer_out = staged_finish(out_halves, staged_route(out_halves), near)
        input_grad = staged_finish(in_halves, staged_route(in_halves), near)
    else:
        *in_blocks, gate_delta, up_delta = gate_up(range(half), delta_tile, deltas, "input_grads")
        gate_grad = weight_grad(tok, gate_delta, keep_gate, "gate_grad")
        up_grad = weight_grad(tok, up_delta, keep_up, "up_grad")
        down_grad = weight_grad(hidden, cot, keep_down, "down_grad")
        layer_out, input_grad = direct_scatter(out_blocks, n), direct_scatter(in_blocks, n)
    return layer_out, input_grad, gate_grad, up_grad, down_grad


def solution(mesh):
    rows = P(("grp", "dp"), "tp")
    return jax.shard_map(
        shards,
        mesh=mesh,
        in_specs=(
            rows,
            rows,
            P("dp", "tp"),
            P("dp", "tp"),
            P("tp", "dp"),
            P(None, "tp"),
            P(None, "tp"),
            P("tp", None),
        ),
        out_specs=(rows, rows, rows, rows, P(("grp", "tp"), "dp")),
        check_vma=False,
    )
```
